32 devices in a mesh: groups: 2 (over y), chan: 8 (over z, x), tm: 2 (over core).
Axes of the slice: x: 2, y: 2, z: 4, core: 2. Of those that a mesh axis runs over, the one named last changes fastest.
Arguments:
- strain: bfloat16 [1024, 16384], P(('groups', 'chan'), 'tm'), parts along dimension 0, may hold values from -500 to 500, as said below
- taps: float32 [64], replicated, may hold values from -0.75 to 0.75
- offsets: int32 [16, 2], P(('groups', 'chan')), parts along dimension 0, may hold values from 1 to 4, as said below
- valid: int32 [16], P(('groups', 'chan')), parts along dimension 0, may hold values from 32 to 64, as said below
Outputs:
- corr: float32 [1024, 2, 512], P(('groups', 'chan'), 'tm'), parts along dimension 0
The draws below stay inside these ranges and needn't reach their ends.
There are 2 independent parts, one for each index of `groups`. The reference program is written for one: setup_inputs(seed, part) draws one part's arguments, and reference() takes and returns one part's arrays. A program takes and returns all parts, laid end to end along the dimension named above; an argument that names none is the same for every part. Nothing has to cross between parts.
Inputs may be any that keep to these rules, and one draw needn't show every extreme that they name: strain samples; scales differ between channels and between stretches of time. The 2 offsets of a block differ from one another; the partner of block b at offset o is block b + o, and a partner past the last block contributes zeros. `valid`: channels of a block at positions from this count on are dead.
All inputs are finite; a program needn't handle non-finite values.
Results may differ from the reference program's by a relative error of at most 0.017.
Values may be sent and summed in bfloat16 or wider, within the bound.
A program may use at most 64 MiB of HBM per device.

```python
import math
import jax
import jax.numpy as jnp
from jax import lax

CH_DEV = 64
NFFT = 1024
LAGS = 512
TAPS = 64
MAXOFF = 4
NPAIR = 2
NBLK = 8
CHANNELS = 512
NSEG = 16
SAMPLES = 16384


def draw_strain(key, part):
    base_key, chan_key, time_key = jax.random.split(key, 3)
    piece = min(128, NFFT)
    pieces = SAMPLES // piece
    chan_scale = jnp.exp(jax.random.uniform(chan_key, (CHANNELS, 1, 1), jnp.float32, 0.0, math.log(10.0)))
    time_scale = jnp.exp(jax.random.uniform(time_key, (1, pieces, 1), jnp.float32, 0.0, math.log(10.0)))
    noise = jnp.clip(jax.random.normal(base_key, (CHANNELS, pieces, piece), jnp.float32), -5.0, 5.0)
    return (noise * chan_scale * time_scale).reshape(CHANNELS, SAMPLES).astype(jnp.bfloat16)


def draw_offsets(key, part):
    first_key, rest_key = jax.random.split(jax.random.fold_in(key, 11))
    rotation = jax.random.randint(first_key, (), 0, MAXOFF)
    block_ids = jnp.arange(NBLK, dtype=jnp.int32)
    first = (block_ids + rotation) % MAXOFF
    row_keys = jax.random.split(rest_key, NBLK)
    others = jax.vmap(lambda row_key: jax.random.permutation(row_key, MAXOFF - 1))(row_keys)[:, :NPAIR - 1]
    rest = (first[:, None] + 1 + others) % MAXOFF
    return (jnp.concatenate([first[:, None], rest], axis=1) + 1).astype(jnp.int32)


def draw_valid(key, part):
    count_key, full_key = jax.random.split(jax.random.fold_in(key, 23))
    counts = jax.random.randint(count_key, (NBLK,), CH_DEV // 2, CH_DEV + 1)
    full_block = jax.random.randint(full_key, (), 0, NBLK)
    return counts.at[full_block].set(CH_DEV).astype(jnp.int32)


def bell_draw(rng, shape, spread, reach, kind=jnp.bfloat16):
    drawn = spread * jax.random.normal(rng, shape, jnp.float32)
    return jnp.clip(drawn, min=-reach, max=reach).astype(kind)


def setup_inputs(seed: int = 0, part: int = 0) -> dict:
    key_of = jax.random.split(jax.random.key(seed), 5)
    part_splits = jax.random.split(jax.random.fold_in(key_of[4], part), 5)
    return {
        "strain": draw_strain(jax.random.fold_in(jax.random.fold_in(key_of[4], part), 71), part),
        "taps": bell_draw(key_of[1], (TAPS,), TAPS ** -0.5, 0.75, jnp.float32),
        "offsets": draw_offsets(jax.random.fold_in(jax.random.fold_in(key_of[4], part), 71), part),
        "valid": draw_valid(jax.random.fold_in(jax.random.fold_in(key_of[4], part), 71), part),
    }


def fourier_table(fft_len, bins):
    sample_idx = lax.broadcasted_iota(jnp.int32, (fft_len, bins), 0)
    bin_idx = lax.broadcasted_iota(jnp.int32, (fft_len, bins), 1)
    phase = (sample_idx * bin_idx % fft_len).astype(jnp.float32) * (2.0 * math.pi / fft_len)
    return jnp.concatenate([jnp.cos(phase), -jnp.sin(phase)], axis=1).astype(jnp.bfloat16)

def lag_table(fft_len, bins, lag_count):
    bin_idx = lax.broadcasted_iota(jnp.int32, (bins, lag_count), 0)
    lag_idx = lax.broadcasted_iota(jnp.int32, (bins, lag_count), 1) - lag_count // 2
    phase = (bin_idx * lag_idx % fft_len).astype(jnp.float32) * (2.0 * math.pi / fft_len)
    return jnp.concatenate([jnp.cos(phase), -jnp.sin(phase)], axis=0)

def whiten(spectra, live, bins):
    real_part = spectra[..., :bins]
    imag_part = spectra[..., bins:]
    energy = real_part * real_part + imag_part * imag_part
    power = lax.optimization_barrier(jnp.mean(energy, axis=-1, keepdims=True)) + 1e-06
    factor = live / jnp.sqrt(energy + 0.1 * power)
    return jnp.concatenate([real_part * factor, imag_part * factor], axis=-1).astype(jnp.bfloat16)

def cross_exact(own, partner, bins):
    own_r = own[..., :bins].astype(jnp.float32)
    own_i = own[..., bins:].astype(jnp.float32)
    part_r = partner[..., :bins].astype(jnp.float32)
    part_i = partner[..., bins:].astype(jnp.float32)
    cross_r = lax.optimization_barrier(jnp.sum(own_r * part_r + own_i * part_i, axis=0))
    cross_i = lax.optimization_barrier(jnp.sum(own_i * part_r - own_r * part_i, axis=0))
    return jnp.concatenate([cross_r, cross_i], axis=-1)

def reference(strain, taps, offsets, valid):
    bins = NFFT // 2
    table = fourier_table(NFFT, bins).astype(jnp.float32)
    inverse = lag_table(NFFT, bins, LAGS)

    def block_panel(block):
        signal = lax.dynamic_slice_in_dim(strain, block * CH_DEV, CH_DEV, 0).astype(jnp.float32)
        padded = jnp.pad(signal, ((0, 0), (TAPS - 1, 0)))
        filtered = jnp.zeros_like(signal)
        for tap_index in range(TAPS):
            begin = TAPS - 1 - tap_index
            filtered = filtered + taps[tap_index] * padded[:, begin:begin + SAMPLES]
        rounded = lax.optimization_barrier(filtered.astype(jnp.bfloat16)).astype(jnp.float32)
        frames = rounded.reshape(CH_DEV, NSEG, NFFT)
        spectra = jnp.einsum('csn,nf->scf', frames, table, precision=lax.Precision.HIGHEST)
        live = (lax.broadcasted_iota(jnp.int32, (1, CH_DEV, 1), 1) < valid[block]).astype(jnp.float32)
        return whiten(spectra, live, bins)
    block_ids = jnp.arange(NBLK, dtype=jnp.int32)
    panels = lax.map(block_panel, block_ids)
    zero_panel = jnp.zeros(panels.shape[1:], jnp.bfloat16)

    def block_corr(block):
        own = lax.dynamic_index_in_dim(panels, block, 0, keepdims=False)
        terms = []
        for pair_slot in range(NPAIR):
            partner_block = block + offsets[block, pair_slot]
            partner = lax.dynamic_index_in_dim(panels, jnp.minimum(partner_block, NBLK - 1).astype(jnp.int32), 0, keepdims=False)
            partner = jnp.where(partner_block < NBLK, partner, zero_panel)
            terms.append(cross_exact(own, partner, bins))
        cross = jnp.stack(terms, axis=1)
        return jnp.einsum('cjf,fl->cjl', cross, inverse, precision=lax.Precision.HIGHEST) / math.sqrt(bins * NSEG)
    corr = lax.map(block_corr, block_ids)
    return corr.reshape(CHANNELS, NPAIR, LAGS)
```

```python
import functools
import math

import jax
import jax.numpy as jnp
import numpy as np
from jax import lax
from jax.experimental import pallas as pl
from jax.experimental.pallas import tpu as pltpu
from jax.sharding import PartitionSpec as P

NFFT = 1024
LAGS = 512
MAXOFF = 4
MESH_ID = pl.DeviceIdType.MESH
SEGS_PER_CHUNK = 2


def host_fourier_table(fft_len, bins):
    sample_idx = np.arange(fft_len)[:, None]
    bin_idx = np.arange(bins)[None, :]
    phase = (2.0 * math.pi / fft_len) * (sample_idx * bin_idx % fft_len)
    return np.concatenate([np.cos(phase), -np.sin(phase)], axis=1).astype(jnp.bfloat16)


def host_lag_table(fft_len, bins, lag_count):
    bin_idx = np.arange(bins)[:, None]
    lag_idx = np.arange(lag_count)[None, :] - lag_count // 2
    phase = (2.0 * math.pi / fft_len) * (bin_idx * lag_idx % fft_len)
    return np.concatenate([np.cos(phase), -np.sin(phase)], axis=0).astype(jnp.bfloat16)


def kernel(
    blocks,
    scale,
    strain_hbm,
    table_hbm,
    inverse_hbm,
    taps_ref,
    offs_ref,
    valid_ref,
    out_ref,
    strain,
    table,
    inverse,
    history,
    offs_all,
    offs_smem,
    acc,
    other_send,
    other_recv,
    ret_send,
    *rest,
):
    channels, length = strain.shape
    fft_len = table.shape[0]
    bins = fft_len // 2
    segments = length // fft_len
    nchunks = segments // SEGS_PER_CHUNK
    positions = channels // blocks
    send = rest[:nchunks]
    recv = rest[nchunks : 2 * nchunks]
    (local_sem, hist_sem, offs_send_sem, offs_recv_sem, send_sem, recv_sem, other_sem,
     ret_send_sem, ret_recv_sem) = rest[2 * nchunks :]

    me = lax.axis_index("chan")
    tm = lax.axis_index("tm")
    steps = range(1, blocks)

    def peer(step):
        return lax.rem(me + step, blocks)

    strain_copy = pltpu.make_async_copy(strain_hbm, strain, local_sem.at[0])
    table_copy = pltpu.make_async_copy(table_hbm, table, local_sem.at[1])
    inverse_copy = pltpu.make_async_copy(inverse_hbm, inverse, local_sem.at[2])
    strain_copy.start()
    table_copy.start()
    inverse_copy.start()

    barrier = pltpu.get_barrier_semaphore()
    for step in steps:
        pl.semaphore_signal(barrier, inc=1, device_id={"chan": peer(step)}, device_id_type=MESH_ID)
    pl.semaphore_signal(barrier, inc=1, device_id={"tm": 1 - tm}, device_id_type=MESH_ID)

    base = jnp.broadcast_to(taps_ref[...], (256, 256))
    fir_full = pltpu.roll(base, 128, 1, stride=1, stride_axis=0)[:, :128]
    fir_high = fir_full.astype(jnp.bfloat16)
    fir_low = (fir_full - fir_high.astype(jnp.float32)).astype(jnp.bfloat16)
    fir = jnp.concatenate([fir_high, fir_low], axis=1)

    pl.semaphore_wait(barrier, blocks)
    strain_copy.wait()

    hist_copy = pltpu.make_async_remote_copy(
        src_ref=strain.at[:, length - 128 :],
        dst_ref=history,
        send_sem=hist_sem.at[0],
        recv_sem=hist_sem.at[1],
        device_id={"tm": 1 - tm},
        device_id_type=MESH_ID,
    )

    @pl.when(tm == 0)
    def _():
        hist_copy.start()
        history[...] = jnp.zeros_like(history)

    offs_copies = []
    for step in steps:
        copy = pltpu.make_async_remote_copy(
            src_ref=offs_ref,
            dst_ref=offs_all.at[me],
            send_sem=offs_send_sem.at[step],
            recv_sem=offs_recv_sem.at[step],
            device_id={"chan": peer(step)},
            device_id_type=MESH_ID,
        )
        copy.start()
        offs_copies.append(copy)
    offs_all[me] = offs_ref[...]

    table_copy.wait()
    live = lax.broadcasted_iota(jnp.int32, (channels, 1), 0) < valid_ref[0]
    live = jnp.where(live, 1.0, 0.0).astype(jnp.float32)
    live = jnp.concatenate([live] * SEGS_PER_CHUNK, axis=0)

    chunk_order = list(range(1, nchunks)) + [0]
    copies = {}
    for chunk in chunk_order:
        first = chunk * SEGS_PER_CHUNK
        windows = []
        for j in range(first * 8, (first + SEGS_PER_CHUNK) * 8):
            if j == 0:

                @pl.when(tm == 1)
                def _():
                    hist_copy.wait_recv()

                windows.append(jnp.concatenate([history[...], strain[:, :128]], axis=1))
            else:
                windows.append(strain[:, 128 * (j - 1) : 128 * (j + 1)])
        window = jnp.concatenate(windows, axis=0)
        both = jnp.dot(window, fir, preferred_element_type=jnp.float32)
        rounded = (both[:, :128] + both[:, 128:]).astype(jnp.bfloat16)
        frames = jnp.concatenate(
            [
                jnp.concatenate(
                    [
                        rounded[(seg * 8 + j) * channels : (seg * 8 + j + 1) * channels]
                        for j in range(8)
                    ],
                    axis=1,
                )
                for seg in range(SEGS_PER_CHUNK)
            ],
            axis=0,
        )
        spectra = jnp.dot(frames, table[...], preferred_element_type=jnp.float32)
        real_part = spectra[:, :bins]
        imag_part = spectra[:, bins:]
        energy = real_part * real_part + imag_part * imag_part
        power = jnp.mean(energy, axis=1, keepdims=True) + 1e-06
        factor = live * lax.rsqrt(energy + 0.1 * power)
        white_r = real_part * factor
        white_i = imag_part * factor
        for block in range(blocks):
            for part, half in ((white_r, 0), (white_i, 1)):
                rows = jnp.concatenate(
                    [
                        part[seg * channels + block * positions :][:positions]
                        for seg in range(SEGS_PER_CHUNK)
                    ],
                    axis=0,
                )
                send[chunk][block, :, half * bins : (half + 1) * bins] = rows.astype(jnp.bfloat16)
        for step in steps:
            copy = pltpu.make_async_remote_copy(
                src_ref=send[chunk].at[peer(step)],
                dst_ref=recv[chunk].at[me],
                send_sem=send_sem.at[chunk, step],
                recv_sem=recv_sem.at[chunk, step],
                device_id={"chan": peer(step)},
                device_id_type=MESH_ID,
            )
            copy.start()
            copies[chunk, step] = copy
        recv[chunk][me] = send[chunk][me]

    for copy in offs_copies:
        copy.wait()
    offs_copy = pltpu.make_async_copy(offs_all, offs_smem, local_sem.at[3])
    offs_copy.start()
    offs_copy.wait()

    for position, chunk in enumerate(chunk_order):
        for step in steps:
            copies[chunk, step].wait_recv()
        for block in range(blocks):
            own = recv[chunk][block].astype(jnp.float32)
            own_r = own[:, :bins]
            own_i = own[:, bins:]
            for slot in range(2):
                index = jnp.minimum(block + offs_smem[block, 0, slot], blocks - 1)
                partner = recv[chunk][index].astype(jnp.float32)
                part_r = partner[:, :bins]
                part_i = partner[:, bins:]
                cross_r = own_r * part_r + own_i * part_i
                cross_i = own_i * part_r - own_r * part_i
                cross = jnp.concatenate([cross_r, cross_i], axis=1)
                total = cross[:positions]
                for seg in range(1, SEGS_PER_CHUNK):
                    total = total + cross[seg * positions : (seg + 1) * positions]
                rows = pl.ds(block * positions, positions)
                if position:
                    total = total + acc[slot, rows]
                if position == nchunks - 1:
                    inside = block + offs_smem[block, 0, slot] < blocks
                    total = total * jnp.where(inside, 1.0, 0.0).astype(jnp.float32)
                acc[slot, rows] = total

    other_send[...] = acc[1 - tm].astype(jnp.bfloat16)
    other_copy = pltpu.make_async_remote_copy(
        src_ref=other_send,
        dst_ref=other_recv,
        send_sem=other_sem.at[0],
        recv_sem=other_sem.at[1],
        device_id={"tm": 1 - tm},
        device_id_type=MESH_ID,
    )
    other_copy.start()
    inverse_copy.wait()
    for copy in copies.values():
        copy.wait_send()
    other_copy.wait()
    summed = (acc[tm] + other_recv[...].astype(jnp.float32)).astype(jnp.bfloat16)
    corr = jnp.dot(summed, inverse[...], preferred_element_type=jnp.float32) * scale
    for block in range(blocks):
        ret_send[block] = corr[block * positions : (block + 1) * positions]
    ret_copies = []
    for step in steps:
        copy = pltpu.make_async_remote_copy(
            src_ref=ret_send.at[peer(step)],
            dst_ref=out_ref.at[me],
            send_sem=ret_send_sem.at[step],
            recv_sem=ret_recv_sem.at[step],
            device_id={"chan": peer(step)},
            device_id_type=MESH_ID,
        )
        copy.start()
        ret_copies.append(copy)
    out_ref[me] = ret_send[me]

    @pl.when(tm == 0)
    def _():
        hist_copy.wait_send()

    for copy in ret_copies:
        copy.wait()


def exchanged(blocks, strain, taps, offsets, valid):
    channels, length = strain.shape
    bins = NFFT // 2
    segments = length // NFFT
    positions = channels // blocks
    nchunks = segments // SEGS_PER_CHUNK
    scale = 1.0 / math.sqrt(bins * segments * 2)
    ntaps = taps.shape[0]
    base = jnp.pad(taps.reshape(1, ntaps), ((0, 0), (0, 256 - ntaps)))
    offs = jnp.pad(offsets, ((0, 7), (0, 126)))
    vmem = pl.BlockSpec(memory_space=pltpu.VMEM)
    hbm = pl.BlockSpec(memory_space=pl.ANY)
    chunk_buf = pltpu.VMEM((blocks, SEGS_PER_CHUNK * positions, NFFT), jnp.bfloat16)
    dma = pltpu.SemaphoreType.DMA
    out = pl.pallas_call(
        functools.partial(kernel, blocks, scale),
        out_shape=jax.ShapeDtypeStruct((blocks, positions, LAGS), jnp.float32),
        in_specs=[hbm, hbm, hbm, vmem, vmem, pl.BlockSpec(memory_space=pltpu.SMEM)],
        out_specs=vmem,
        scratch_shapes=[
            pltpu.VMEM((channels, length), jnp.bfloat16),
            pltpu.VMEM((NFFT, NFFT), jnp.bfloat16),
            pltpu.VMEM((NFFT, LAGS), jnp.bfloat16),
            pltpu.VMEM((channels, 128), jnp.bfloat16),
            pltpu.VMEM((blocks, 8, 128), jnp.int32),
            pltpu.SMEM((blocks, 8, 128), jnp.int32),
            pltpu.VMEM((2, channels, NFFT), jnp.float32),
            pltpu.VMEM((channels, NFFT), jnp.bfloat16),
            pltpu.VMEM((channels, NFFT), jnp.bfloat16),
            pltpu.VMEM((blocks, positions, LAGS), jnp.float32),
            *[chunk_buf] * (2 * nchunks),
            dma((4,)),
            dma((2,)),
            dma((blocks,)),
            dma((blocks,)),
            dma((nchunks, blocks)),
            dma((nchunks, blocks)),
            dma((2,)),
            dma((blocks,)),
            dma((blocks,)),
        ],
        compiler_params=pltpu.CompilerParams(
            collective_id=0, has_side_effects=True, vmem_limit_bytes=40 * 1024 * 1024
        ),
    )(
        strain,
        jnp.asarray(host_fourier_table(NFFT, bins)),
        jnp.asarray(host_lag_table(NFFT, bins, LAGS)),
        base,
        offs,
        valid,
    )
    return out.reshape(channels, 1, LAGS)


def passed_along(value, axis, steps):
    count = lax.axis_size(axis)
    first, last = (max(0, -steps), min(count, count - steps))
    return lax.ppermute(value, axis, [(source, source + steps) for source in range(first, last)])


def fourier_table(fft_len, bins):
    sample_idx = lax.broadcasted_iota(jnp.int32, (fft_len, bins), 0)
    bin_idx = lax.broadcasted_iota(jnp.int32, (fft_len, bins), 1)
    phase = (sample_idx * bin_idx % fft_len).astype(jnp.float32) * (2.0 * math.pi / fft_len)
    return jnp.concatenate([jnp.cos(phase), -jnp.sin(phase)], axis=1).astype(jnp.bfloat16)


def lag_table(fft_len, bins, lag_count):
    bin_idx = lax.broadcasted_iota(jnp.int32, (bins, lag_count), 0)
    lag_idx = lax.broadcasted_iota(jnp.int32, (bins, lag_count), 1) - lag_count // 2
    phase = (bin_idx * lag_idx % fft_len).astype(jnp.float32) * (2.0 * math.pi / fft_len)
    return jnp.concatenate([jnp.cos(phase), -jnp.sin(phase)], axis=0)


def fir_matrix(taps, block_len):
    ntaps = taps.shape[0]
    rows = block_len + ntaps
    row_idx = lax.broadcasted_iota(jnp.int32, (rows, block_len), 0)
    col_idx = lax.broadcasted_iota(jnp.int32, (rows, block_len), 1)
    tap_idx = col_idx + ntaps - row_idx
    onehot = (tap_idx[:, :, None] == lax.broadcasted_iota(jnp.int32, (1, 1, ntaps), 2)).astype(
        jnp.float32
    )
    return jnp.dot(
        onehot.reshape(rows * block_len, ntaps), taps, precision=lax.Precision.HIGHEST
    ).reshape(rows, block_len)


def whiten(spectra, live, bins):
    real_part = spectra[..., :bins]
    imag_part = spectra[..., bins:]
    energy = real_part * real_part + imag_part * imag_part
    power = jnp.mean(energy, axis=-1, keepdims=True) + 1e-06
    factor = live / jnp.sqrt(energy + 0.1 * power)
    return jnp.concatenate([real_part * factor, imag_part * factor], axis=-1).astype(jnp.bfloat16)


def cross_spectrum(own, partner, bins):
    own_r = own[..., :bins]
    own_i = own[..., bins:]
    part_r = partner[..., :bins]
    part_i = partner[..., bins:]

    def contract(left, right):
        return jnp.einsum("scf,scf->cf", left, right, preferred_element_type=jnp.float32)

    cross_r = contract(own_r, part_r) + contract(own_i, part_i)
    cross_i = contract(own_i, part_r) - contract(own_r, part_i)
    return jnp.concatenate([cross_r, cross_i], axis=-1)


def on_device(strain, taps, offsets, valid):
    channels, length = strain.shape
    ntaps = taps.shape[0]
    fft_len = NFFT
    bins = fft_len // 2
    block_len = min(128, fft_len)
    history = passed_along(strain[:, length - ntaps :], "tm", 1)
    padded = jnp.concatenate([history, strain], axis=1)
    nblocks = length // block_len
    lower = padded[:, :length].reshape(channels, nblocks, block_len)
    upper = strain.reshape(channels, nblocks, block_len)[:, :, block_len - ntaps :]
    window = jnp.concatenate([lower, upper], axis=2)
    fir_full = fir_matrix(taps, block_len)
    fir_high = fir_full.astype(jnp.bfloat16)
    fir_low = (fir_full - fir_high.astype(jnp.float32)).astype(jnp.bfloat16)
    filtered = jnp.einsum("cjw,ws->cjs", window, fir_high, preferred_element_type=jnp.float32)
    filtered = filtered + jnp.einsum(
        "cjw,ws->cjs", window, fir_low, preferred_element_type=jnp.float32
    )
    rounded = filtered.reshape(channels, length).astype(jnp.bfloat16)
    segments = length // fft_len
    frames = rounded.reshape(channels, segments, fft_len)
    spectra = jnp.einsum(
        "csn,nf->scf", frames, fourier_table(fft_len, bins), preferred_element_type=jnp.float32
    )
    live = (lax.broadcasted_iota(jnp.int32, (1, channels, 1), 1) < valid[0]).astype(jnp.float32)
    panel = whiten(spectra, live, bins)
    received = []
    for distance in range(1, MAXOFF + 1):
        received.append(passed_along(panel, "chan", -distance))
    stacked = jnp.stack(received, axis=0)
    pairs = offsets.shape[1]
    terms = []
    for pair_slot in range(pairs):
        partner = lax.dynamic_index_in_dim(stacked, offsets[0, pair_slot] - 1, 0, keepdims=False)
        terms.append(cross_spectrum(panel, partner, bins))
    cross = jnp.stack(terms, axis=1)
    inverse = lag_table(fft_len, bins, LAGS)
    denominator = math.sqrt(bins * segments * lax.axis_size("tm"))
    summed = lax.psum_scatter(
        cross.astype(jnp.bfloat16), "tm", scatter_dimension=1, tiled=True
    ).astype(jnp.float32)
    corr = jnp.einsum("cjf,fl->cjl", summed, inverse, precision=lax.Precision.HIGHEST) / denominator
    return corr


def solution(mesh):
    in_specs = (
        P(("groups", "chan"), "tm"),
        P(),
        P(("groups", "chan"), None),
        P(("groups", "chan")),
    )
    out_specs = P(("groups", "chan"), "tm", None)
    blocks = mesh.shape["chan"]
    body = on_device
    if blocks == 8 and mesh.shape["tm"] == 2:
        body = functools.partial(exchanged, blocks)
    return jax.shard_map(
        body, mesh=mesh, in_specs=in_specs, out_specs=out_specs, check_vma=False
    )
```

```python
import functools
import math

import jax
import jax.numpy as jnp
import numpy as np
from jax import lax
from jax.experimental import pallas as pl
from jax.experimental.pallas import tpu as pltpu
from jax.sharding import PartitionSpec as P

NFFT = 1024
LAGS = 512
MAXOFF = 4
MESH_ID = pl.DeviceIdType.MESH
SEGS_PER_CHUNK = 2


def host_fourier_table(fft_len, bins):
    sample_idx = np.arange(fft_len)[:, None]
    bin_idx = np.arange(bins)[None, :]
    phase = (2.0 * math.pi / fft_len) * (sample_idx * bin_idx % fft_len)
    return np.concatenate([np.cos(phase), -np.sin(phase)], axis=1).astype(jnp.bfloat16)


def host_lag_table(fft_len, bins, lag_count):
    bin_idx = np.arange(bins)[:, None]
    lag_idx = np.arange(lag_count)[None, :] - lag_count // 2
    phase = (2.0 * math.pi / fft_len) * (bin_idx * lag_idx % fft_len)
    return np.concatenate([np.cos(phase), -np.sin(phase)], axis=0).astype(jnp.bfloat16)


def kernel(
    blocks,
    scale,
    strain_hbm,
    table_hbm,
    inverse_hbm,
    taps_ref,
    offs_ref,
    valid_ref,
    out_ref,
    strain,
    table,
    inverse,
    history,
    base,
    info,
    info_all,
    info_smem,
    acc,
    white_first,
    ret_send,
    ret_recv,
    *rest,
):
    channels, length = strain.shape
    fft_len = table.shape[0]
    bins = fft_len // 2
    segments = length // fft_len
    nchunks = segments // SEGS_PER_CHUNK
    positions = channels // blocks
    ntaps = taps_ref.shape[1]
    send = rest[:nchunks]
    recv = rest[nchunks : 2 * nchunks]
    (local_sem, hist_sem, info_send_sem, info_recv_sem, send_sem, recv_sem,
     ret_send_sem, ret_recv_sem) = rest[2 * nchunks :]

    me = lax.axis_index("chan")
    tm = lax.axis_index("tm")
    steps = range(1, blocks)
    ret_steps = [(step, flip) for step in range(blocks) for flip in range(2) if step or flip]

    def peer(step):
        return lax.rem(me + step, blocks)

    def core(flip):
        return 1 - tm if flip else tm

    barrier = pltpu.get_barrier_semaphore()
    for step, flip in ret_steps:
        pl.semaphore_signal(
            barrier, inc=1, device_id={"chan": peer(step), "tm": core(flip)}, device_id_type=MESH_ID
        )

    strain_copy = pltpu.make_async_copy(strain_hbm, strain, local_sem.at[0])
    table_copy = pltpu.make_async_copy(table_hbm, table, local_sem.at[1])
    inverse_copy = pltpu.make_async_copy(inverse_hbm, inverse, local_sem.at[2])
    strain_copy.start()
    table_copy.start()
    inverse_copy.start()

    base[...] = jnp.zeros_like(base)
    base[:, :ntaps] = taps_ref[...]
    fir_full = pltpu.roll(
        jnp.broadcast_to(base[...], (256, 256)), 128, 1, stride=1, stride_axis=0
    )[:, :128]
    fir_high = fir_full.astype(jnp.bfloat16)
    fir_low = (fir_full - fir_high.astype(jnp.float32)).astype(jnp.bfloat16)
    fir = jnp.concatenate([fir_high, fir_low], axis=1)

    lane = lax.broadcasted_iota(jnp.int32, info.shape, 1)
    info[...] = jnp.where(
        lane == 0, offs_ref[0, 0], jnp.where(lane == 1, offs_ref[0, 1], valid_ref[0])
    )
    live = lax.broadcasted_iota(jnp.int32, (channels, 1), 0) < valid_ref[0]
    live = jnp.where(live, 1.0, 0.0).astype(jnp.float32)
    live = jnp.concatenate([live] * SEGS_PER_CHUNK, axis=0)

    def filtered_frames(chunk):
        first = chunk * SEGS_PER_CHUNK
        windows = []
        for j in range(first * 8, (first + SEGS_PER_CHUNK) * 8):
            if j == 0:
                windows.append(jnp.concatenate([history[...], strain[:, :128]], axis=1))
            else:
                windows.append(strain[:, 128 * (j - 1) : 128 * (j + 1)])
        window = jnp.concatenate(windows, axis=0)
        both = jnp.dot(window, fir, preferred_element_type=jnp.float32)
        flat = both[:, :128] + both[:, 128:]
        return jnp.concatenate(
            [
                jnp.concatenate(
                    [flat[(seg * 8 + j) * channels :][:channels] for j in range(8)], axis=1
                )
                for seg in range(SEGS_PER_CHUNK)
            ],
            axis=0,
        )

    def whitened(frames, row_live):
        spectra = jnp.dot(frames, table[...], preferred_element_type=jnp.float32)
        real_part = spectra[:, :bins]
        imag_part = spectra[:, bins:]
        energy = real_part * real_part + imag_part * imag_part
        power = jnp.mean(energy, axis=1, keepdims=True) + 1e-06
        factor = row_live * lax.rsqrt(energy + 0.1 * power)
        return real_part * factor, imag_part * factor

    def by_block(part, block):
        return jnp.concatenate(
            [
                part[seg * channels + block * positions :][:positions]
                for seg in range(SEGS_PER_CHUNK)
            ],
            axis=0,
        ).astype(jnp.bfloat16)

    chunk_order = list(range(1, nchunks)) + [0]
    copies = {}

    def send_chunk(chunk):
        for step in steps:
            copy = pltpu.make_async_remote_copy(
                src_ref=send[chunk].at[peer(step)],
                dst_ref=recv[chunk].at[me],
                send_sem=send_sem.at[chunk, step],
                recv_sem=recv_sem.at[chunk, step],
                device_id={"chan": peer(step)},
                device_id_type=MESH_ID,
            )
            copy.start()
            copies[chunk, step] = copy
        recv[chunk][me] = send[chunk][me]

    opening = chunk_order[0]
    strain_copy.wait()
    frames = filtered_frames(opening)
    for block in range(blocks):
        send[opening][block] = by_block(frames, block)

    pl.semaphore_wait(barrier, len(ret_steps))
    send_chunk(opening)

    hist_copy = pltpu.make_async_remote_copy(
        src_ref=strain.at[:, length - 128 :],
        dst_ref=history,
        send_sem=hist_sem.at[0],
        recv_sem=hist_sem.at[1],
        device_id={"tm": 1 - tm},
        device_id_type=MESH_ID,
    )

    @pl.when(tm == 0)
    def _():
        hist_copy.start()
        history[...] = jnp.zeros_like(history)

    info_copies = []
    for step in steps:
        copy = pltpu.make_async_remote_copy(
            src_ref=info,
            dst_ref=info_all.at[me],
            send_sem=info_send_sem.at[step],
            recv_sem=info_recv_sem.at[step],
            device_id={"chan": peer(step)},
            device_id_type=MESH_ID,
        )
        copy.start()
        info_copies.append(copy)
    info_all[me] = info[...]

    table_copy.wait()
    for chunk in chunk_order[1:]:
        if chunk == 0:

            @pl.when(tm == 1)
            def _():
                hist_copy.wait_recv()

        frames = filtered_frames(chunk).astype(jnp.bfloat16)
        white_r, white_i = whitened(frames, live)
        for block in range(blocks):
            send[chunk][block, :, :bins] = by_block(white_r, block)
            send[chunk][block, :, bins:] = by_block(white_i, block)
        send_chunk(chunk)

    for copy in info_copies:
        copy.wait()
    info_copy = pltpu.make_async_copy(info_all, info_smem, local_sem.at[3])
    info_copy.start()
    info_copy.wait()

    for position, chunk in enumerate(chunk_order):
        for step in steps:
            copies[chunk, step].wait_recv()
        panel = recv[chunk]
        if chunk == opening:
            index = lax.broadcasted_iota(jnp.int32, (positions, 1), 0) + me * positions
            row_live = []
            for block in range(blocks):
                alive = jnp.where(index < info_smem[block, 0, 2], 1.0, 0.0).astype(jnp.float32)
                row_live.extend([alive] * SEGS_PER_CHUNK)
            frames = jnp.concatenate([panel[block] for block in range(blocks)], axis=0)
            white_r, white_i = whitened(frames, jnp.concatenate(row_live, axis=0))
            panel = white_first
            rows = SEGS_PER_CHUNK * positions
            for block in range(blocks):
                panel[block, :, :bins] = white_r[block * rows :][:rows].astype(jnp.bfloat16)
                panel[block, :, bins:] = white_i[block * rows :][:rows].astype(jnp.bfloat16)
        for block in range(blocks):
            own = panel[block].astype(jnp.float32)
            own_r = own[:, :bins]
            own_i = own[:, bins:]
            for slot in range(2):
                index = jnp.minimum(block + info_smem[block, 0, slot], blocks - 1)
                partner = panel[index].astype(jnp.float32)
                part_r = partner[:, :bins]
                part_i = partner[:, bins:]
                cross_r = own_r * part_r + own_i * part_i
                cross_i = own_i * part_r - own_r * part_i
                cross = jnp.concatenate([cross_r, cross_i], axis=1)
                total = cross[:positions]
                for seg in range(1, SEGS_PER_CHUNK):
                    total = total + cross[seg * positions : (seg + 1) * positions]
                rows = pl.ds(slot * channels + block * positions, positions)
                if position:
                    total = total + acc[rows]
                if position == nchunks - 1:
                    inside = block + info_smem[block, 0, slot] < blocks
                    total = total * jnp.where(inside, scale, 0.0).astype(jnp.float32)
                acc[rows] = total
        if position == 0:
            inverse_copy.wait()

    corr = jnp.dot(
        acc[...].astype(jnp.bfloat16), inverse[...], preferred_element_type=jnp.float32
    )
    half = corr.shape[1] // 2
    for slot in range(2):
        for block in range(blocks):
            rows = corr[slot * channels + block * positions :][:positions]
            rows = jnp.concatenate([rows[:, :half], rows[:, half:]], axis=0)
            ret_send[slot, block] = rows.astype(jnp.bfloat16)
    ret_copies = []
    for step, flip in ret_steps:
        copy = pltpu.make_async_remote_copy(
            src_ref=ret_send.at[core(flip), peer(step)],
            dst_ref=ret_recv.at[tm, me],
            send_sem=ret_send_sem.at[step, flip],
            recv_sem=ret_recv_sem.at[step, flip],
            device_id={"chan": peer(step), "tm": core(flip)},
            device_id_type=MESH_ID,
        )
        copy.start()
        ret_copies.append(copy)
    ret_recv[tm, me] = ret_send[tm, me]

    @pl.when(tm == 0)
    def _():
        hist_copy.wait_send()

    for copy in copies.values():
        copy.wait_send()
    for copy in ret_copies:
        copy.wait()
    for block in range(blocks):
        rows = ret_recv[0, block].astype(jnp.float32) + ret_recv[1, block].astype(jnp.float32)
        out_ref[block, :, :half] = rows[:positions]
        out_ref[block, :, half:] = rows[positions:]


def exchanged(blocks, strain, taps, offsets, valid):
    channels, length = strain.shape
    bins = NFFT // 2
    segments = length // NFFT
    positions = channels // blocks
    nchunks = segments // SEGS_PER_CHUNK
    scale = 1.0 / math.sqrt(bins * segments * 2)
    vmem = pl.BlockSpec(memory_space=pltpu.VMEM)
    smem = pl.BlockSpec(memory_space=pltpu.SMEM)
    hbm = pl.BlockSpec(memory_space=pl.ANY)
    chunk_buf = pltpu.VMEM((blocks, SEGS_PER_CHUNK * positions, NFFT), jnp.bfloat16)
    ret_buf = pltpu.VMEM((2, blocks, 2 * positions, LAGS // 2), jnp.bfloat16)
    dma = pltpu.SemaphoreType.DMA
    out = pl.pallas_call(
        functools.partial(kernel, blocks, scale),
        out_shape=jax.ShapeDtypeStruct((blocks, positions, LAGS), jnp.float32),
        in_specs=[hbm, hbm, hbm, vmem, smem, smem],
        out_specs=vmem,
        scratch_shapes=[
            pltpu.VMEM((channels, length), jnp.bfloat16),
            pltpu.VMEM((NFFT, NFFT), jnp.bfloat16),
            pltpu.VMEM((NFFT, LAGS), jnp.bfloat16),
            pltpu.VMEM((channels, 128), jnp.bfloat16),
            pltpu.VMEM((1, 256), jnp.float32),
            pltpu.VMEM((8, 128), jnp.int32),
            pltpu.VMEM((blocks, 8, 128), jnp.int32),
            pltpu.SMEM((blocks, 8, 128), jnp.int32),
            pltpu.VMEM((2 * channels, NFFT), jnp.float32),
            chunk_buf,
            ret_buf,
            ret_buf,
            *[chunk_buf] * (2 * nchunks),
            dma((4,)),
            dma((2,)),
            dma((blocks,)),
            dma((blocks,)),
            dma((nchunks, blocks)),
            dma((nchunks, blocks)),
            dma((blocks, 2)),
            dma((blocks, 2)),
        ],
        compiler_params=pltpu.CompilerParams(
            collective_id=0, has_side_effects=True, vmem_limit_bytes=60 * 1024 * 1024
        ),
    )(
        strain,
        jnp.asarray(host_fourier_table(NFFT, bins)),
        jnp.asarray(host_lag_table(NFFT, bins, LAGS)),
        taps.reshape(1, -1),
        offsets,
        valid,
    )
    return out.reshape(channels, 1, LAGS)


def passed_along(value, axis, steps):
    count = lax.axis_size(axis)
    first, last = (max(0, -steps), min(count, count - steps))
    return lax.ppermute(value, axis, [(source, source + steps) for source in range(first, last)])


def fourier_table(fft_len, bins):
    sample_idx = lax.broadcasted_iota(jnp.int32, (fft_len, bins), 0)
    bin_idx = lax.broadcasted_iota(jnp.int32, (fft_len, bins), 1)
    phase = (sample_idx * bin_idx % fft_len).astype(jnp.float32) * (2.0 * math.pi / fft_len)
    return jnp.concatenate([jnp.cos(phase), -jnp.sin(phase)], axis=1).astype(jnp.bfloat16)


def lag_table(fft_len, bins, lag_count):
    bin_idx = lax.broadcasted_iota(jnp.int32, (bins, lag_count), 0)
    lag_idx = lax.broadcasted_iota(jnp.int32, (bins, lag_count), 1) - lag_count // 2
    phase = (bin_idx * lag_idx % fft_len).astype(jnp.float32) * (2.0 * math.pi / fft_len)
    return jnp.concatenate([jnp.cos(phase), -jnp.sin(phase)], axis=0)


def fir_matrix(taps, block_len):
    ntaps = taps.shape[0]
    rows = block_len + ntaps
    row_idx = lax.broadcasted_iota(jnp.int32, (rows, block_len), 0)
    col_idx = lax.broadcasted_iota(jnp.int32, (rows, block_len), 1)
    tap_idx = col_idx + ntaps - row_idx
    onehot = (tap_idx[:, :, None] == lax.broadcasted_iota(jnp.int32, (1, 1, ntaps), 2)).astype(
        jnp.float32
    )
    return jnp.dot(
        onehot.reshape(rows * block_len, ntaps), taps, precision=lax.Precision.HIGHEST
    ).reshape(rows, block_len)


def whiten(spectra, live, bins):
    real_part = spectra[..., :bins]
    imag_part = spectra[..., bins:]
    energy = real_part * real_part + imag_part * imag_part
    power = jnp.mean(energy, axis=-1, keepdims=True) + 1e-06
    factor = live / jnp.sqrt(energy + 0.1 * power)
    return jnp.concatenate([real_part * factor, imag_part * factor], axis=-1).astype(jnp.bfloat16)


def cross_spectrum(own, partner, bins):
    own_r = own[..., :bins]
    own_i = own[..., bins:]
    part_r = partner[..., :bins]
    part_i = partner[..., bins:]

    def contract(left, right):
        return jnp.einsum("scf,scf->cf", left, right, preferred_element_type=jnp.float32)

    cross_r = contract(own_r, part_r) + contract(own_i, part_i)
    cross_i = contract(own_i, part_r) - contract(own_r, part_i)
    return jnp.concatenate([cross_r, cross_i], axis=-1)


def on_device(strain, taps, offsets, valid):
    channels, length = strain.shape
    ntaps = taps.shape[0]
    fft_len = NFFT
    bins = fft_len // 2
    block_len = min(128, fft_len)
    history = passed_along(strain[:, length - ntaps :], "tm", 1)
    padded = jnp.concatenate([history, strain], axis=1)
    nblocks = length // block_len
    lower = padded[:, :length].reshape(channels, nblocks, block_len)
    upper = strain.reshape(channels, nblocks, block_len)[:, :, block_len - ntaps :]
    window = jnp.concatenate([lower, upper], axis=2)
    fir_full = fir_matrix(taps, block_len)
    fir_high = fir_full.astype(jnp.bfloat16)
    fir_low = (fir_full - fir_high.astype(jnp.float32)).astype(jnp.bfloat16)
    filtered = jnp.einsum("cjw,ws->cjs", window, fir_high, preferred_element_type=jnp.float32)
    filtered = filtered + jnp.einsum(
        "cjw,ws->cjs", window, fir_low, preferred_element_type=jnp.float32
    )
    rounded = filtered.reshape(channels, length).astype(jnp.bfloat16)
    segments = length // fft_len
    frames = rounded.reshape(channels, segments, fft_len)
    spectra = jnp.einsum(
        "csn,nf->scf", frames, fourier_table(fft_len, bins), preferred_element_type=jnp.float32
    )
    live = (lax.broadcasted_iota(jnp.int32, (1, channels, 1), 1) < valid[0]).astype(jnp.float32)
    panel = whiten(spectra, live, bins)
    received = []
    for distance in range(1, MAXOFF + 1):
        received.append(passed_along(panel, "chan", -distance))
    stacked = jnp.stack(received, axis=0)
    pairs = offsets.shape[1]
    terms = []
    for pair_slot in range(pairs):
        partner = lax.dynamic_index_in_dim(stacked, offsets[0, pair_slot] - 1, 0, keepdims=False)
        terms.append(cross_spectrum(panel, partner, bins))
    cross = jnp.stack(terms, axis=1)
    inverse = lag_table(fft_len, bins, LAGS)
    denominator = math.sqrt(bins * segments * lax.axis_size("tm"))
    summed = lax.psum_scatter(
        cross.astype(jnp.bfloat16), "tm", scatter_dimension=1, tiled=True
    ).astype(jnp.float32)
    corr = jnp.einsum("cjf,fl->cjl", summed, inverse, precision=lax.Precision.HIGHEST) / denominator
    return corr


def solution(mesh):
    in_specs = (
        P(("groups", "chan"), "tm"),
        P(),
        P(("groups", "chan"), None),
        P(("groups", "chan")),
    )
    out_specs = P(("groups", "chan"), "tm", None)
    blocks = mesh.shape["chan"]
    body = on_device
    if blocks == 8 and mesh.shape["tm"] == 2:
        body = functools.partial(exchanged, blocks)
    return jax.shard_map(
        body, mesh=mesh, in_specs=in_specs, out_specs=out_specs, check_vma=False
    )
```

```python
import functools
import math

import jax
import jax.numpy as jnp
import numpy as np
from jax import lax
from jax.experimental import pallas as pl
from jax.experimental.pallas import tpu as pltpu
from jax.sharding import PartitionSpec as P

NFFT = 1024
LAGS = 512
MAXOFF = 4
MESH_ID = pl.DeviceIdType.MESH
SEGS_PER_CHUNK = 2


def host_fourier_table(fft_len, bins):
    sample_idx = np.arange(fft_len)[:, None]
    bin_idx = np.arange(bins)[None, :]
    phase = (2.0 * math.pi / fft_len) * (sample_idx * bin_idx % fft_len)
    return np.concatenate([np.cos(phase), -np.sin(phase)], axis=1).astype(jnp.bfloat16)


def host_lag_table(fft_len, bins, lag_count):
    bin_idx = np.arange(bins)[:, None]
    lag_idx = np.arange(lag_count)[None, :] - lag_count // 2
    phase = (2.0 * math.pi / fft_len) * (bin_idx * lag_idx % fft_len)
    return np.concatenate([np.cos(phase), -np.sin(phase)], axis=0).astype(jnp.bfloat16)


def kernel(
    blocks,
    scale,
    strain_hbm,
    table_hbm,
    inverse_hbm,
    taps_ref,
    offs_ref,
    valid_ref,
    out_ref,
    strain,
    table,
    inverse,
    history,
    base,
    info,
    info_all,
    info_smem,
    acc,
    white_first,
    ret_send,
    ret_recv,
    *rest,
):
    channels, length = strain.shape
    fft_len = table.shape[0]
    bins = fft_len // 2
    segments = length // fft_len
    nchunks = segments // SEGS_PER_CHUNK
    positions = channels // blocks
    ntaps = taps_ref.shape[1]
    send = rest[:nchunks]
    recv = rest[nchunks : 2 * nchunks]
    (local_sem, hist_sem, info_send_sem, info_recv_sem, send_sem, recv_sem,
     ret_send_sem, ret_recv_sem) = rest[2 * nchunks :]

    me = lax.axis_index("chan")
    tm = lax.axis_index("tm")
    steps = (7, 6, 5, 4, 3, 2, 1)
    ret_steps = [(step, flip) for step in range(blocks - 1, -1, -1) for flip in range(2) if step or flip]

    def peer(step):
        return me ^ step

    def core(flip):
        return 1 - tm if flip else tm

    barrier = pltpu.get_barrier_semaphore()
    for step, flip in ret_steps:
        pl.semaphore_signal(
            barrier, inc=1, device_id={"chan": peer(step), "tm": core(flip)}, device_id_type=MESH_ID
        )

    strain_copy = pltpu.make_async_copy(strain_hbm, strain, local_sem.at[0])
    table_copy = pltpu.make_async_copy(table_hbm, table, local_sem.at[1])
    inverse_copy = pltpu.make_async_copy(inverse_hbm, inverse, local_sem.at[2])
    strain_copy.start()
    table_copy.start()
    inverse_copy.start()

    base[...] = jnp.zeros_like(base)
    base[:, :ntaps] = taps_ref[...]
    fir_full = pltpu.roll(
        jnp.broadcast_to(base[...], (256, 256)), 128, 1, stride=1, stride_axis=0
    )[:, :128]
    fir_high = fir_full.astype(jnp.bfloat16)
    fir_low = (fir_full - fir_high.astype(jnp.float32)).astype(jnp.bfloat16)
    fir = jnp.concatenate([fir_high, fir_low], axis=1)

    lane = lax.broadcasted_iota(jnp.int32, info.shape, 1)
    info[...] = jnp.where(
        lane == 0, offs_ref[0, 0], jnp.where(lane == 1, offs_ref[0, 1], valid_ref[0])
    )
    live = lax.broadcasted_iota(jnp.int32, (channels, 1), 0) < valid_ref[0]
    live = jnp.where(live, 1.0, 0.0).astype(jnp.float32)
    live = jnp.concatenate([live] * SEGS_PER_CHUNK, axis=0)

    def filtered_frames(chunk):
        first = chunk * SEGS_PER_CHUNK
        windows = []
        for j in range(first * 8, (first + SEGS_PER_CHUNK) * 8):
            if j == 0:
                windows.append(jnp.concatenate([history[...], strain[:, :128]], axis=1))
            else:
                windows.append(strain[:, 128 * (j - 1) : 128 * (j + 1)])
        window = jnp.concatenate(windows, axis=0)
        both = jnp.dot(window, fir, preferred_element_type=jnp.float32)
        flat = both[:, :128] + both[:, 128:]
        return jnp.concatenate(
            [
                jnp.concatenate(
                    [flat[(seg * 8 + j) * channels :][:channels] for j in range(8)], axis=1
                )
                for seg in range(SEGS_PER_CHUNK)
            ],
            axis=0,
        )

    def whitened(frames, row_live):
        spectra = jnp.dot(frames, table[...], preferred_element_type=jnp.float32)
        real_part = spectra[:, :bins]
        imag_part = spectra[:, bins:]
        energy = real_part * real_part + imag_part * imag_part
        power = jnp.mean(energy, axis=1, keepdims=True) + 1e-06
        factor = row_live * lax.rsqrt(energy + 0.1 * power)
        return real_part * factor, imag_part * factor

    def by_block(part, block):
        return jnp.concatenate(
            [
                part[seg * channels + block * positions :][:positions]
                for seg in range(SEGS_PER_CHUNK)
            ],
            axis=0,
        ).astype(jnp.bfloat16)

    chunk_order = list(range(1, nchunks)) + [0]
    copies = {}

    def send_chunk(chunk):
        for step in steps:
            copy = pltpu.make_async_remote_copy(
                src_ref=send[chunk].at[peer(step)],
                dst_ref=recv[chunk].at[me],
                send_sem=send_sem.at[chunk, step],
                recv_sem=recv_sem.at[chunk, step],
                device_id={"chan": peer(step)},
                device_id_type=MESH_ID,
            )
            copy.start()
            copies[chunk, step] = copy
        recv[chunk][me] = send[chunk][me]

    opening = chunk_order[0]
    strain_copy.wait()
    frames = filtered_frames(opening)
    for block in range(blocks):
        send[opening][block] = by_block(frames, block)

    pl.semaphore_wait(barrier, len(ret_steps))
    send_chunk(opening)

    hist_copy = pltpu.make_async_remote_copy(
        src_ref=strain.at[:, length - 128 :],
        dst_ref=history,
        send_sem=hist_sem.at[0],
        recv_sem=hist_sem.at[1],
        device_id={"tm": 1 - tm},
        device_id_type=MESH_ID,
    )

    @pl.when(tm == 0)
    def _():
        hist_copy.start()
        history[...] = jnp.zeros_like(history)

    info_copies = []
    for step in steps:
        copy = pltpu.make_async_remote_copy(
            src_ref=info,
            dst_ref=info_all.at[me],
            send_sem=info_send_sem.at[step],
            recv_sem=info_recv_sem.at[step],
            device_id={"chan": peer(step)},
            device_id_type=MESH_ID,
        )
        copy.start()
        info_copies.append(copy)
    info_all[me] = info[...]

    table_copy.wait()
    for chunk in chunk_order[1:]:
        if chunk == 0:

            @pl.when(tm == 1)
            def _():
                hist_copy.wait_recv()

        frames = filtered_frames(chunk).astype(jnp.bfloat16)
        white_r, white_i = whitened(frames, live)
        for block in range(blocks):
            send[chunk][block, :, :bins] = by_block(white_r, block)
            send[chunk][block, :, bins:] = by_block(white_i, block)
        send_chunk(chunk)

    for copy in info_copies:
        copy.wait()
    info_copy = pltpu.make_async_copy(info_all, info_smem, local_sem.at[3])
    info_copy.start()
    info_copy.wait()

    for position, chunk in enumerate(chunk_order):
        for step in steps:
            copies[chunk, step].wait_recv()
        panel = recv[chunk]
        if chunk == opening:
            index = lax.broadcasted_iota(jnp.int32, (positions, 1), 0) + me * positions
            row_live = []
            for block in range(blocks):
                alive = jnp.where(index < info_smem[block, 0, 2], 1.0, 0.0).astype(jnp.float32)
                row_live.extend([alive] * SEGS_PER_CHUNK)
            frames = jnp.concatenate([panel[block] for block in range(blocks)], axis=0)
            white_r, white_i = whitened(frames, jnp.concatenate(row_live, axis=0))
            panel = white_first
            rows = SEGS_PER_CHUNK * positions
            for block in range(blocks):
                panel[block, :, :bins] = white_r[block * rows :][:rows].astype(jnp.bfloat16)
                panel[block, :, bins:] = white_i[block * rows :][:rows].astype(jnp.bfloat16)
        for block in range(blocks):
            own = panel[block].astype(jnp.float32)
            own_r = own[:, :bins]
            own_i = own[:, bins:]
            for slot in range(2):
                index = jnp.minimum(block + info_smem[block, 0, slot], blocks - 1)
                partner = panel[index].astype(jnp.float32)
                part_r = partner[:, :bins]
                part_i = partner[:, bins:]
                cross_r = own_r * part_r + own_i * part_i
                cross_i = own_i * part_r - own_r * part_i
                cross = jnp.concatenate([cross_r, cross_i], axis=1)
                total = cross[:positions]
                for seg in range(1, SEGS_PER_CHUNK):
                    total = total + cross[seg * positions : (seg + 1) * positions]
                rows = pl.ds(slot * channels + block * positions, positions)
                if position:
                    total = total + acc[rows]
                if position == nchunks - 1:
                    inside = block + info_smem[block, 0, slot] < blocks
                    total = total * jnp.where(inside, scale, 0.0).astype(jnp.float32)
                acc[rows] = total
        if position == 0:
            inverse_copy.wait()

    corr = jnp.dot(
        acc[...].astype(jnp.bfloat16), inverse[...], preferred_element_type=jnp.float32
    )
    half = corr.shape[1] // 2
    for slot in range(2):
        for block in range(blocks):
            rows = corr[slot * channels + block * positions :][:positions]
            rows = jnp.concatenate([rows[:, :half], rows[:, half:]], axis=0)
            ret_send[slot, block] = rows.astype(jnp.bfloat16)
    ret_copies = []
    for step, flip in ret_steps:
        copy = pltpu.make_async_remote_copy(
            src_ref=ret_send.at[core(flip), peer(step)],
            dst_ref=ret_recv.at[tm, me],
            send_sem=ret_send_sem.at[step, flip],
            recv_sem=ret_recv_sem.at[step, flip],
            device_id={"chan": peer(step), "tm": core(flip)},
            device_id_type=MESH_ID,
        )
        copy.start()
        ret_copies.append(copy)
    ret_recv[tm, me] = ret_send[tm, me]

    @pl.when(tm == 0)
    def _():
        hist_copy.wait_send()

    for copy in copies.values():
        copy.wait_send()
    for copy in ret_copies:
        copy.wait()
    for block in range(blocks):
        rows = ret_recv[0, block].astype(jnp.float32) + ret_recv[1, block].astype(jnp.float32)
        out_ref[block, :, :half] = rows[:positions]
        out_ref[block, :, half:] = rows[positions:]


def exchanged(blocks, strain, taps, offsets, valid):
    channels, length = strain.shape
    bins = NFFT // 2
    segments = length // NFFT
    positions = channels // blocks
    nchunks = segments // SEGS_PER_CHUNK
    scale = 1.0 / math.sqrt(bins * segments * 2)
    vmem = pl.BlockSpec(memory_space=pltpu.VMEM)
    smem = pl.BlockSpec(memory_space=pltpu.SMEM)
    hbm = pl.BlockSpec(memory_space=pl.ANY)
    chunk_buf = pltpu.VMEM((blocks, SEGS_PER_CHUNK * positions, NFFT), jnp.bfloat16)
    ret_buf = pltpu.VMEM((2, blocks, 2 * positions, LAGS // 2), jnp.bfloat16)
    dma = pltpu.SemaphoreType.DMA
    out = pl.pallas_call(
        functools.partial(kernel, blocks, scale),
        out_shape=jax.ShapeDtypeStruct((blocks, positions, LAGS), jnp.float32),
        in_specs=[hbm, hbm, hbm, vmem, smem, smem],
        out_specs=vmem,
        scratch_shapes=[
            pltpu.VMEM((channels, length), jnp.bfloat16),
            pltpu.VMEM((NFFT, NFFT), jnp.bfloat16),
            pltpu.VMEM((NFFT, LAGS), jnp.bfloat16),
            pltpu.VMEM((channels, 128), jnp.bfloat16),
            pltpu.VMEM((1, 256), jnp.float32),
            pltpu.VMEM((8, 128), jnp.int32),
            pltpu.VMEM((blocks, 8, 128), jnp.int32),
            pltpu.SMEM((blocks, 8, 128), jnp.int32),
            pltpu.VMEM((2 * channels, NFFT), jnp.float32),
            chunk_buf,
            ret_buf,
            ret_buf,
            *[chunk_buf] * (2 * nchunks),
            dma((4,)),
            dma((2,)),
            dma((blocks,)),
            dma((blocks,)),
            dma((nchunks, blocks)),
            dma((nchunks, blocks)),
            dma((blocks, 2)),
            dma((blocks, 2)),
        ],
        compiler_params=pltpu.CompilerParams(
            collective_id=0, has_side_effects=True, vmem_limit_bytes=60 * 1024 * 1024
        ),
    )(
        strain,
        jnp.asarray(host_fourier_table(NFFT, bins)),
        jnp.asarray(host_lag_table(NFFT, bins, LAGS)),
        taps.reshape(1, -1),
        offsets,
        valid,
    )
    return out.reshape(channels, 1, LAGS)


def passed_along(value, axis, steps):
    count = lax.axis_size(axis)
    first, last = (max(0, -steps), min(count, count - steps))
    return lax.ppermute(value, axis, [(source, source + steps) for source in range(first, last)])


def fourier_table(fft_len, bins):
    sample_idx = lax.broadcasted_iota(jnp.int32, (fft_len, bins), 0)
    bin_idx = lax.broadcasted_iota(jnp.int32, (fft_len, bins), 1)
    phase = (sample_idx * bin_idx % fft_len).astype(jnp.float32) * (2.0 * math.pi / fft_len)
    return jnp.concatenate([jnp.cos(phase), -jnp.sin(phase)], axis=1).astype(jnp.bfloat16)


def lag_table(fft_len, bins, lag_count):
    bin_idx = lax.broadcasted_iota(jnp.int32, (bins, lag_count), 0)
    lag_idx = lax.broadcasted_iota(jnp.int32, (bins, lag_count), 1) - lag_count // 2
    phase = (bin_idx * lag_idx % fft_len).astype(jnp.float32) * (2.0 * math.pi / fft_len)
    return jnp.concatenate([jnp.cos(phase), -jnp.sin(phase)], axis=0)


def fir_matrix(taps, block_len):
    ntaps = taps.shape[0]
    rows = block_len + ntaps
    row_idx = lax.broadcasted_iota(jnp.int32, (rows, block_len), 0)
    col_idx = lax.broadcasted_iota(jnp.int32, (rows, block_len), 1)
    tap_idx = col_idx + ntaps - row_idx
    onehot = (tap_idx[:, :, None] == lax.broadcasted_iota(jnp.int32, (1, 1, ntaps), 2)).astype(
        jnp.float32
    )
    return jnp.dot(
        onehot.reshape(rows * block_len, ntaps), taps, precision=lax.Precision.HIGHEST
    ).reshape(rows, block_len)


def whiten(spectra, live, bins):
    real_part = spectra[..., :bins]
    imag_part = spectra[..., bins:]
    energy = real_part * real_part + imag_part * imag_part
    power = jnp.mean(energy, axis=-1, keepdims=True) + 1e-06
    factor = live / jnp.sqrt(energy + 0.1 * power)
    return jnp.concatenate([real_part * factor, imag_part * factor], axis=-1).astype(jnp.bfloat16)


def cross_spectrum(own, partner, bins):
    own_r = own[..., :bins]
    own_i = own[..., bins:]
    part_r = partner[..., :bins]
    part_i = partner[..., bins:]

    def contract(left, right):
        return jnp.einsum("scf,scf->cf", left, right, preferred_element_type=jnp.float32)

    cross_r = contract(own_r, part_r) + contract(own_i, part_i)
    cross_i = contract(own_i, part_r) - contract(own_r, part_i)
    return jnp.concatenate([cross_r, cross_i], axis=-1)


def on_device(strain, taps, offsets, valid):
    channels, length = strain.shape
    ntaps = taps.shape[0]
    fft_len = NFFT
    bins = fft_len // 2
    block_len = min(128, fft_len)
    history = passed_along(strain[:, length - ntaps :], "tm", 1)
    padded = jnp.concatenate([history, strain], axis=1)
    nblocks = length // block_len
    lower = padded[:, :length].reshape(channels, nblocks, block_len)
    upper = strain.reshape(channels, nblocks, block_len)[:, :, block_len - ntaps :]
    window = jnp.concatenate([lower, upper], axis=2)
    fir_full = fir_matrix(taps, block_len)
    fir_high = fir_full.astype(jnp.bfloat16)
    fir_low = (fir_full - fir_high.astype(jnp.float32)).astype(jnp.bfloat16)
    filtered = jnp.einsum("cjw,ws->cjs", window, fir_high, preferred_element_type=jnp.float32)
    filtered = filtered + jnp.einsum(
        "cjw,ws->cjs", window, fir_low, preferred_element_type=jnp.float32
    )
    rounded = filtered.reshape(channels, length).astype(jnp.bfloat16)
    segments = length // fft_len
    frames = rounded.reshape(channels, segments, fft_len)
    spectra = jnp.einsum(
        "csn,nf->scf", frames, fourier_table(fft_len, bins), preferred_element_type=jnp.float32
    )
    live = (lax.broadcasted_iota(jnp.int32, (1, channels, 1), 1) < valid[0]).astype(jnp.float32)
    panel = whiten(spectra, live, bins)
    received = []
    for distance in range(1, MAXOFF + 1):
        received.append(passed_along(panel, "chan", -distance))
    stacked = jnp.stack(received, axis=0)
    pairs = offsets.shape[1]
    terms = []
    for pair_slot in range(pairs):
        partner = lax.dynamic_index_in_dim(stacked, offsets[0, pair_slot] - 1, 0, keepdims=False)
        terms.append(cross_spectrum(panel, partner, bins))
    cross = jnp.stack(terms, axis=1)
    inverse = lag_table(fft_len, bins, LAGS)
    denominator = math.sqrt(bins * segments * lax.axis_size("tm"))
    summed = lax.psum_scatter(
        cross.astype(jnp.bfloat16), "tm", scatter_dimension=1, tiled=True
    ).astype(jnp.float32)
    corr = jnp.einsum("cjf,fl->cjl", summed, inverse, precision=lax.Precision.HIGHEST) / denominator
    return corr


def solution(mesh):
    in_specs = (
        P(("groups", "chan"), "tm"),
        P(),
        P(("groups", "chan"), None),
        P(("groups", "chan")),
    )
    out_specs = P(("groups", "chan"), "tm", None)
    blocks = mesh.shape["chan"]
    body = on_device
    if blocks == 8 and mesh.shape["tm"] == 2:
        body = functools.partial(exchanged, blocks)
    return jax.shard_map(
        body, mesh=mesh, in_specs=in_specs, out_specs=out_specs, check_vma=False
    )
```
